32 devices in a mesh: row: 16 (over z, y, core), col: 2 (over x).
Axes of the slice: x: 2, y: 2, z: 4, core: 2. Of those that a mesh axis runs over, the one named last changes fastest.
Arguments:
- alignment: bfloat16 [64, 512, 64], P(None, ('col', 'row')), may hold values from -6 to 6
- pair_rep: bfloat16 [512, 512, 128], P('row', 'col'), may hold values from -128 to 128
- outer_left: bfloat16 [64, 32], replicated, may hold values from -0.75 to 0.75
- outer_right: bfloat16 [64, 32], replicated, may hold values from -0.75 to 0.75
- outer_proj: bfloat16 [1024, 128], replicated, may hold values from -1.5 to 1.5
- outer_bias: float32 [128], replicated, may hold values from -3 to 3
- average_value: bfloat16 [64, 256], replicated, may hold values from -0.75 to 0.75
- average_gate: bfloat16 [64, 256], replicated, may hold values from -0.75 to 0.75
- average_logit: bfloat16 [128, 8], replicated, may hold values from -28 to 28
- average_out: bfloat16 [256, 64], replicated, may hold values from -1 to 1
- triangle_proj: bfloat16 [128, 512], replicated, may hold values from -0.5 to 0.5
- triangle_bias: bfloat16 [128, 4], replicated, may hold values from -0.5 to 0.5
Outputs:
- pair_new: bfloat16 [512, 512, 128], P('row', 'col')
- alignment_update: bfloat16 [64, 512, 64], P(None, ('row', 'col'))
- triangle_inputs: bfloat16 [512, 512, 512], P(('col', 'row'))
- edge_bias: bfloat16 [4, 512, 512], P(None, ('col', 'row'))
The draws below stay inside these ranges and needn't reach their ends.
All inputs are finite; a program needn't handle non-finite values.
Results may differ from the reference program's by a relative error of at most 0.02.
The reference program's roundings to bfloat16 on the way count: a program that leaves them out, or rounds other values in their place, can miss the bound.
Values may be sent and summed in bfloat16 or wider, within the bound.
A program may use at most 64 MiB of HBM per device.

```python
import math
import jax
import jax.numpy as jnp
from jax import lax

CM = 64
CZ = 128
OPM_C = 32
PWA_H = 8
PWA_C = 32
TRI_H = 4
TRI_C = 32
SEQS = 64
ROW_TOK = 32
TOKENS = 512
N_ROW = 16


def draw_average_logit(key, part):
    strength = jnp.exp(jax.random.uniform(jax.random.fold_in(key, 102), (PWA_H,), jnp.float32, math.log(0.7), math.log(4.0)))
    noise_part = jax.random.normal(jax.random.fold_in(key, 103), (CZ, PWA_H), jnp.float32)
    return (noise_part * strength[None, :] / math.sqrt(CZ)).astype(jnp.bfloat16)


def draw_pair_rep(key, part):
    noise_part = jnp.clip(jax.random.normal(jax.random.fold_in(key, 201), (TOKENS, TOKENS, CZ), jnp.float32), -6.0, 6.0)
    return noise_part.astype(jnp.bfloat16)


def block_scale(key, extent, pieces, low, high):
    gain = 1.0
    for dim, shards_of in pieces:
        heights = jax.random.uniform(jax.random.fold_in(jax.random.fold_in(key, 6), dim), (shards_of,), jnp.float32, low / len(pieces), high / len(pieces))
        gain = gain * jnp.repeat(jnp.exp(heights), extent[dim] // shards_of).reshape((-1,) + (1,) * (len(extent) - 1 - dim))
    return gain


def scatter_about(key, dims, width, most, cuts=(), kind=jnp.bfloat16):
    array = width * jax.random.normal(key, dims, jnp.float32)
    if cuts:
        array = array * block_scale(key, dims, cuts, -0.22, 0.18)
    return jnp.clip(array, -most, most).astype(kind)


def setup_inputs(seed: int = 0) -> dict:
    key_list = jax.random.split(jax.random.key(seed), 13)
    alignment = scatter_about(key_list[0], (SEQS, TOKENS, CM), 1.0, 6.0, ((1, 32),))
    pair_rep = draw_pair_rep(jax.random.fold_in(key_list[12], 71), 0)
    outer_left = scatter_about(key_list[2], (CM, OPM_C), CM ** -0.5, 0.75)
    outer_right = scatter_about(key_list[3], (CM, OPM_C), CM ** -0.5, 0.75)
    outer_proj = scatter_about(key_list[4], (OPM_C * OPM_C, CZ), (OPM_C * OPM_C // SEQS) ** -0.5, 1.5)
    outer_bias = scatter_about(key_list[5], (CZ,), 0.5, 3.0, (), jnp.float32)
    average_value = scatter_about(key_list[6], (CM, PWA_H * PWA_C), CM ** -0.5, 0.75)
    average_gate = scatter_about(key_list[7], (CM, PWA_H * PWA_C), CM ** -0.5, 0.75)
    average_logit = draw_average_logit(jax.random.fold_in(key_list[12], 71), 0)
    average_out = scatter_about(key_list[9], (PWA_H * PWA_C, CM), PWA_C ** -0.5, 1.0)
    triangle_proj = scatter_about(key_list[10], (CZ, 4 * TRI_H * TRI_C), CZ ** -0.5, 0.5)
    triangle_bias = scatter_about(key_list[11], (CZ, TRI_H), CZ ** -0.5, 0.5)
    return {"alignment": alignment, "pair_rep": pair_rep, "outer_left": outer_left, "outer_right": outer_right, "outer_proj": outer_proj, "outer_bias": outer_bias, "average_value": average_value, "average_gate": average_gate, "average_logit": average_logit, "average_out": average_out, "triangle_proj": triangle_proj, "triangle_bias": triangle_bias}


def standardize(values):
    widened = values.astype(jnp.float32)
    centered = widened - lax.optimization_barrier(jnp.mean(widened, axis=-1, keepdims=True))
    spread = lax.optimization_barrier(jnp.mean(centered * centered, axis=-1, keepdims=True))
    return centered * lax.rsqrt(spread + 1e-05)

def reference(alignment, pair_rep, outer_left, outer_right, outer_proj, outer_bias, average_value, average_gate, average_logit, average_out, triangle_proj, triangle_bias):
    alignment_layer_norm = standardize(alignment).astype(jnp.bfloat16)
    left_factor = jnp.dot(alignment_layer_norm, outer_left, preferred_element_type=jnp.float32).astype(jnp.bfloat16)
    right_factor = jnp.dot(alignment_layer_norm, outer_right, preferred_element_type=jnp.float32).astype(jnp.bfloat16)
    right_wide = right_factor.astype(jnp.float32)
    left_blocks = jnp.transpose(left_factor.reshape(SEQS, N_ROW, ROW_TOK, OPM_C), (1, 0, 2, 3))
    pair_blocks = pair_rep.reshape(N_ROW, ROW_TOK, TOKENS, CZ)

    def pair_block(block_items):
        left_block, pair_rows = block_items
        outer_mean = jnp.einsum('sic,sjd->ijcd', left_block.astype(jnp.float32), right_wide) / SEQS
        outer_mean = outer_mean.reshape(ROW_TOK, TOKENS, OPM_C * OPM_C).astype(jnp.bfloat16)
        update = jnp.dot(outer_mean, outer_proj, preferred_element_type=jnp.float32)
        return (pair_rows.astype(jnp.float32) + update + outer_bias).astype(jnp.bfloat16)
    pair_new = lax.map(pair_block, (left_blocks, pair_blocks)).reshape(TOKENS, TOKENS, CZ)
    pair_norm = standardize(pair_new).astype(jnp.bfloat16)
    logits = jnp.dot(pair_norm, average_logit, preferred_element_type=jnp.float32)
    weights = jnp.exp(logits - lax.optimization_barrier(jnp.max(logits, axis=1, keepdims=True))).astype(jnp.bfloat16)
    weights_wide = weights.astype(jnp.float32)
    denom = lax.optimization_barrier(jnp.sum(weights_wide, axis=1))
    values = jnp.dot(alignment_layer_norm, average_value, preferred_element_type=jnp.float32).astype(jnp.bfloat16)
    values = values.reshape(SEQS, TOKENS, PWA_H, PWA_C)
    gate_vals = jax.nn.sigmoid(jnp.dot(alignment_layer_norm, average_gate, preferred_element_type=jnp.float32))
    gate_vals = gate_vals.reshape(SEQS, TOKENS, PWA_H, PWA_C)
    numer = jnp.einsum('ijh,sjhc->sihc', weights_wide, values.astype(jnp.float32))
    gated = (gate_vals * numer / denom[None, :, :, None]).reshape(SEQS, TOKENS, PWA_H * PWA_C)
    alignment_update = jnp.dot(gated, average_out.astype(jnp.float32), precision=lax.Precision.HIGHEST).astype(jnp.bfloat16)
    turned = jnp.swapaxes(pair_norm, 0, 1).reshape(N_ROW, ROW_TOK, TOKENS, CZ)
    split_at = 3 * TRI_H * TRI_C

    def triangle_block(block_rows):
        projected = jnp.dot(block_rows, triangle_proj, preferred_element_type=jnp.float32)
        inputs = jnp.concatenate([projected[..., :split_at], jax.nn.sigmoid(projected[..., split_at:])], axis=-1).astype(jnp.bfloat16)
        bias_rows = jnp.dot(block_rows, triangle_bias, preferred_element_type=jnp.float32).astype(jnp.bfloat16)
        return (inputs, bias_rows)
    triangle_blocks, bias_blocks = lax.map(triangle_block, turned)
    triangle_inputs = triangle_blocks.reshape(TOKENS, TOKENS, 4 * TRI_H * TRI_C)
    edge_bias = jnp.transpose(bias_blocks.reshape(TOKENS, TOKENS, TRI_H), (2, 0, 1))
    return (pair_new, alignment_update, triangle_inputs, edge_bias)
```

```python
import functools
import jax
import jax.numpy as jnp
from jax import lax
from jax.sharding import PartitionSpec as P
from jax.experimental import pallas as pl
from jax.experimental.pallas import tpu as pltpu

MESH = pl.DeviceIdType.MESH
BF16 = jnp.bfloat16
F32 = jnp.float32
NT = (((1,), (1,)), ((), ()))


def broadcast(shard, axis, root):
    mine = lax.axis_index(axis) == root
    return lax.psum(jnp.where(mine, shard, jnp.zeros_like(shard)), axis)


def standardize(values):
    widened = values.astype(jnp.float32)
    centered = widened - jnp.mean(widened, axis=-1, keepdims=True)
    spread = jnp.mean(centered * centered, axis=-1, keepdims=True)
    return centered * lax.rsqrt(spread + 1e-05)


def per_device(
    alignment,
    pair_rep,
    outer_left,
    outer_right,
    outer_proj,
    outer_bias,
    average_value,
    average_gate,
    average_logit,
    average_out,
    triangle_proj,
    triangle_bias,
):
    row_devices = lax.axis_size("row")
    col_devices = lax.axis_size("col")
    local_row_index = lax.axis_index("row")
    col_index = lax.axis_index("col")
    sequence_count, slab_length, alignment_channel_width = alignment.shape
    row_window, cols_tile, pair_width = pair_rep.shape
    factor_width = outer_left.shape[1]
    head_count = average_logit.shape[1]
    value_width = average_value.shape[1]
    head_width = value_width // head_count
    alignment_layer_norm = standardize(alignment).astype(jnp.bfloat16)
    normalized_flat_rows = alignment_layer_norm.reshape(
        sequence_count, slab_length * alignment_channel_width
    )
    normalized_columns = lax.all_gather(normalized_flat_rows, "row", axis=1, tiled=True)
    norm_wide = normalized_columns.reshape(sequence_count, cols_tile, alignment_channel_width)
    right_cols = jnp.dot(norm_wide, outer_right, preferred_element_type=jnp.float32).astype(
        jnp.bfloat16
    )
    value_cols = jnp.dot(norm_wide, average_value, preferred_element_type=jnp.float32).astype(
        jnp.bfloat16
    )
    group_member_count = row_devices // col_devices
    start_position = local_row_index % group_member_count * (row_window * alignment_channel_width)
    local_rows = lax.dynamic_slice_in_dim(
        normalized_columns, start_position, row_window * alignment_channel_width, 1
    )
    norm_rows = broadcast(local_rows, "col", local_row_index // group_member_count).reshape(
        sequence_count, row_window, alignment_channel_width
    )
    left_rows = jnp.dot(norm_rows, outer_left, preferred_element_type=jnp.float32).astype(
        jnp.bfloat16
    )
    row_block = 8
    block_count = row_window // row_block
    left_blocks = jnp.transpose(
        left_rows.reshape(sequence_count, block_count, row_block * factor_width), (1, 0, 2)
    )
    right_flat = right_cols.reshape(sequence_count, cols_tile * factor_width)

    def pair_block(block_items):
        left_flat, pair_rows = block_items
        outer_sum = lax.dot_general(
            left_flat, right_flat, (((0,), (0,)), ((), ())), preferred_element_type=jnp.float32
        )
        outer_sum = jnp.transpose(
            outer_sum.reshape(row_block, factor_width, cols_tile, factor_width), (0, 2, 1, 3)
        )
        outer_mean = (
            outer_sum.reshape(row_block, cols_tile, factor_width * factor_width) / sequence_count
        ).astype(jnp.bfloat16)
        update = jnp.dot(outer_mean, outer_proj, preferred_element_type=jnp.float32)
        return (pair_rows.astype(jnp.float32) + update + outer_bias).astype(jnp.bfloat16)

    pair_new = lax.map(
        pair_block, (left_blocks, pair_rep.reshape(block_count, row_block, cols_tile, pair_width))
    )
    pair_new = pair_new.reshape(row_window, cols_tile, pair_width)
    pair_norm = standardize(pair_new).astype(jnp.bfloat16)
    logits = jnp.einsum("ijc,ch->hij", pair_norm, average_logit, preferred_element_type=jnp.float32)
    peak_values = lax.pmax(jnp.max(logits, axis=2), "col")
    weights = jnp.exp(logits - peak_values[:, :, None]).astype(jnp.bfloat16)
    denom_part = jnp.sum(weights.astype(jnp.float32), axis=2)
    value_heads = value_cols.reshape(sequence_count, cols_tile, head_count, head_width)
    numer_part = jnp.einsum(
        "hij,sjhc->ishc", weights, value_heads, preferred_element_type=jnp.float32
    )
    numer_part = numer_part.reshape(row_window, sequence_count, value_width)
    out_wide = average_out.astype(jnp.float32)
    numer_sub, denom_sub = (
        lax.psum_scatter(
            numer_part.astype(jnp.bfloat16), "col", scatter_dimension=0, tiled=True
        ).astype(jnp.float32),
        lax.psum_scatter(
            denom_part.astype(jnp.bfloat16), "col", scatter_dimension=1, tiled=True
        ).astype(jnp.float32),
    )
    sub_len = numer_sub.shape[0]
    norm_sub = lax.dynamic_slice_in_dim(norm_rows, col_index * sub_len, sub_len, 1)
    gate_vals = jax.nn.sigmoid(jnp.dot(norm_sub, average_gate, preferred_element_type=jnp.float32))
    gate_vals = gate_vals.reshape(sequence_count, sub_len, head_count, head_width)
    numer_moved = jnp.transpose(
        numer_sub.reshape(sub_len, sequence_count, head_count, head_width), (1, 0, 2, 3)
    )
    gated_vals = (gate_vals * numer_moved / jnp.transpose(denom_sub)[None, :, :, None]).reshape(
        sequence_count, sub_len, value_width
    )
    alignment_update = jnp.dot(gated_vals, out_wide, precision=lax.Precision.HIGHEST).astype(
        jnp.bfloat16
    )
    piece_len = cols_tile // row_devices
    shaped = pair_norm.reshape(row_window, row_devices, piece_len, pair_width)
    split_at = 3 * (triangle_proj.shape[1] // 4)
    turned = lax.all_to_all(shaped, "row", split_axis=1, concat_axis=0, tiled=True)[:, 0]
    projected = jnp.einsum("jic,cd->ijd", turned, triangle_proj, preferred_element_type=jnp.float32)
    inputs = jnp.concatenate(
        [projected[..., :split_at], jax.nn.sigmoid(projected[..., split_at:])], axis=-1
    ).astype(jnp.bfloat16)
    bias_rows = jnp.einsum(
        "jic,ch->ihj", turned, triangle_bias, preferred_element_type=jnp.float32
    ).astype(jnp.bfloat16)
    triangle_inputs, bias_rows = (inputs, bias_rows)
    edge_bias = jnp.transpose(bias_rows, (1, 0, 2))
    return (pair_new, alignment_update, triangle_inputs, edge_bias)


def dot_nt(a, b):
    return lax.dot_general(a, b, NT, preferred_element_type=F32)


def dot_nn(a, b):
    return jnp.dot(a, b, preferred_element_type=F32)


def gather_kernel(rows_n, align_ref, cols_ref, rows_ref, own, send_sem, recv_sem, row_sem):
    half, slab = own.shape[0], own.shape[1]
    r, c = lax.axis_index("row"), lax.axis_index("col")
    far = rows_n // 4
    a, b, e = r // 4, (r // 2) % 2, r % 2

    def place(a_, b_, e_):
        return (a_ * 4 + b_ * 2 + e_, c)

    across = (a, 1 - b, e)
    beside = (a, b, 1 - e)
    distant = [(lax.rem(a + k, far), b, e) for k in range(1, far)]
    shard = c * rows_n + r
    owner = (shard // 2, 1 - c)
    source_col = (2 * r) // rows_n
    source_row = lax.rem(2 * r, rows_n)
    barrier = pltpu.get_barrier_semaphore()
    for spot in distant + [across, beside]:
        pl.semaphore_signal(barrier, inc=1, device_id=place(*spot), device_id_type=MESH)

    @pl.when(source_col != c)
    def _():
        for k in range(2):
            pl.semaphore_signal(
                barrier, inc=1, device_id=(source_row + k, source_col), device_id_type=MESH
            )

    wide = align_ref[...].astype(F32)
    centered = wide - jnp.mean(wide, axis=-1, keepdims=True)
    spread = jnp.mean(centered * centered, axis=-1, keepdims=True)
    norm = centered * lax.rsqrt(spread + 1e-05)
    own[...] = jnp.concatenate([norm[:half], norm[half:]], axis=-1).astype(BF16)
    pl.semaphore_wait(barrier, far + 2)

    def window(index):
        return cols_ref.at[:, pl.ds(pl.multiple_of(index * slab, slab), slab), :]

    started = []

    def send(src, index, target):
        copy = pltpu.make_async_remote_copy(
            src_ref=src,
            dst_ref=window(index),
            send_sem=send_sem.at[len(started)],
            recv_sem=recv_sem.at[index],
            device_id=target,
            device_id_type=MESH,
        )
        copy.start()
        started.append(copy)

    def arrived(index):
        pltpu.make_async_remote_copy(
            src_ref=own,
            dst_ref=window(index),
            send_sem=send_sem.at[0],
            recv_sem=recv_sem.at[index],
            device_id=place(*beside),
            device_id_type=MESH,
        ).wait_recv()

    for spot in distant:
        send(own, r, place(*spot))
    send(own, r, place(*across))
    send(own, r, place(*beside))
    row_copy = pltpu.make_async_remote_copy(
        src_ref=own,
        dst_ref=rows_ref.at[:, pl.ds(pl.multiple_of(lax.rem(shard, 2) * slab, slab), slab), :],
        send_sem=send_sem.at[len(started)],
        recv_sem=row_sem.at[lax.rem(shard, 2)],
        device_id=owner,
        device_id_type=MESH,
    )
    row_copy.start()
    started.append(row_copy)
    window(r)[...] = own[...]

    def index_of(spot):
        return spot[0] * 4 + spot[1] * 2 + spot[2]

    def forward(spot, both):
        index = index_of(spot)
        arrived(index)
        if both:
            send(window(index), index, place(*across))
        send(window(index), index, place(*beside))

    forward(across, False)
    for k in range(far - 1, 0, -1):
        spot = (lax.rem(a + k, far), b, e)
        forward(spot, True)
    for k in range(far - 1, 0, -1):
        forward((lax.rem(a + k, far), 1 - b, e), False)
    for k in [0] + list(range(far - 1, 0, -1)):
        for flip in range(2):
            arrived(index_of((lax.rem(a + k, far), b if flip == 0 else 1 - b, 1 - e)))

    @pl.when(source_col == c)
    def _():
        rows_ref[...] = cols_ref[
            :, pl.ds(pl.multiple_of(source_row * slab, 2 * slab), 2 * slab), :
        ]

    @pl.when(source_col != c)
    def _():
        for k in range(2):
            pltpu.make_async_remote_copy(
                src_ref=own,
                dst_ref=rows_ref.at[:, k * slab : (k + 1) * slab, :],
                send_sem=send_sem.at[0],
                recv_sem=row_sem.at[k],
                device_id=owner,
                device_id_type=MESH,
            ).wait_recv()

    for copy in started:
        copy.wait_send()


def pair_kernel(
    rows_n, heads, cols_ref, rows_ref, pair_ref, right_ref, left_ref, proj_ref, bias_ref, value_ref,
    gate_ref, logit_ref, out_ref, new_ref, update_ref, turned_ref, rs, rb, nr, lt, outer, spun, ready,
    lg, num, stat, nsend, nrecv, ssend, srecv, turn_send, turn_recv, local_sem, col_send, col_recv,
):
    half, tile, lanes = cols_ref.shape
    rows = rows_ref.shape[1]
    slab = tile // rows_n
    width = right_ref.shape[0] // 2
    block = 8
    chunk = slab
    span = heads * rows
    r, c = lax.axis_index("row"), lax.axis_index("col")
    barrier = pltpu.get_barrier_semaphore()

    @pl.loop(1, rows_n)
    def _(k):
        pl.semaphore_signal(
            barrier, inc=1, device_id=(lax.rem(r + k, rows_n), c), device_id_type=MESH
        )

    pl.semaphore_signal(barrier, inc=1, device_id=(r, 1 - c), device_id_type=MESH)

    @pl.loop(0, half)
    def _(s):
        res = dot_nt(right_ref[...], cols_ref[s])
        for t in range(tile // 128):
            piece = res[:, t * 128 : (t + 1) * 128]
            rs[t, pl.ds(pl.multiple_of(s * width, width), width), :] = piece[:width]
            rs[t, pl.ds(pl.multiple_of((half + s) * width, width), width), :] = piece[width:]

    for d in range(width):
        for t in range(tile // 128):
            at = d * tile + t * 128
            rb[:, at : at + 128] = rs.at[t][pl.ds(d, 2 * half, stride=width), :].astype(BF16)

    nr[...] = rows_ref[...].astype(F32).reshape(half * rows, lanes)
    for i in range(rows):
        token = nr[pl.ds(i, half, stride=rows), :].astype(BF16)
        res = dot_nt(left_ref[...], token)
        lt[i * width : (i + 1) * width, :] = jnp.concatenate(
            [res[:width], res[width:]], axis=1
        ).astype(BF16)

    def do_block(base, place):
        left = lt[pl.ds(pl.multiple_of(base * width, block * width), block * width), :]
        for d in range(width):
            res = dot_nn(left, rb[:, d * tile : (d + 1) * tile]).astype(BF16)
            outer[:, d * width : (d + 1) * width, :] = res.reshape(block, width, tile)

        @pl.loop(0, block)
        def _(k):
            i = base + k
            update = dot_nn(proj_ref[...], outer[k]).T
            fresh = (pair_ref[i].astype(F32) + update + bias_ref[...]).astype(BF16)
            new_ref[i] = fresh
            wide = fresh.astype(F32)
            centered = wide - jnp.mean(wide, axis=-1, keepdims=True)
            spread = jnp.mean(centered * centered, axis=-1, keepdims=True)
            norm = (centered * lax.rsqrt(spread + 1e-05)).astype(BF16)
            logit = dot_nt(logit_ref[...], norm)
            for t in range(tile // 128):
                lg.at[t][pl.ds(i, heads, stride=rows), :] = logit[:, t * 128 : (t + 1) * 128]
            spun[pl.ds(place + k, tile, stride=chunk), :] = norm.astype(F32)

    def turn(part, k):
        other = lax.rem(r + k, rows_n)
        return pltpu.make_async_remote_copy(
            src_ref=ready.at[part, pl.ds(other * slab, slab)],
            dst_ref=turned_ref.at[
                :, pl.ds(pl.multiple_of(r * rows + part * chunk, chunk), chunk), :
            ],
            send_sem=turn_send.at[part, k],
            recv_sem=turn_recv.at[part, r],
            device_id=(other, c),
            device_id_type=MESH,
        )

    def local_turn(part):
        return pltpu.make_async_copy(
            ready.at[part, pl.ds(r * slab, slab)],
            turned_ref.at[:, pl.ds(pl.multiple_of(r * rows + part * chunk, chunk), chunk), :],
            local_sem.at[part],
        )

    parts = rows // chunk
    for part in range(parts):
        @pl.loop(0, chunk // block)
        def _(n):
            do_block(part * chunk + n * block, n * block)

        ready[part] = spun[...].astype(BF16).reshape(tile, chunk, lanes)
        if part == 0:
            pl.semaphore_wait(barrier, rows_n)
        local_turn(part).start()

        @pl.loop(1, rows_n)
        def _(k):
            turn(part, k).start()

    logits = jnp.concatenate([lg[t] for t in range(tile // 128)], axis=1)
    peak = jnp.max(logits, axis=-1, keepdims=True)
    weights = jnp.exp(logits - peak).astype(BF16)
    groups = 2
    heads_in = heads // groups
    gspan = heads_in * rows
    glanes = value_ref.shape[1] // groups
    each = glanes // heads_in

    def pick(res):
        lane = lax.broadcasted_iota(jnp.int32, (rows, glanes), 1)
        total = res[:rows]
        for h in range(1, heads_in):
            total = jnp.where(lane >= h * each, res[h * rows : (h + 1) * rows], total)
        return total

    ones = jnp.ones((tile, glanes), BF16)
    for g in range(groups):
        stat[0, :, g * glanes : (g + 1) * glanes] = pick(
            jnp.broadcast_to(peak[g * gspan : (g + 1) * gspan], (gspan, glanes))
        )
        stat[1, :, g * glanes : (g + 1) * glanes] = pick(
            dot_nn(weights[g * gspan : (g + 1) * gspan], ones)
        )

    @pl.loop(0, half)
    def _(s):
        values = dot_nn(cols_ref[s], value_ref[...]).astype(BF16)
        for g in range(groups):
            num[s, :, g * glanes : (g + 1) * glanes] = pick(
                dot_nn(
                    weights[g * gspan : (g + 1) * gspan], values[:, g * glanes : (g + 1) * glanes]
                )
            )

    mine = pl.ds(pl.multiple_of(c * slab, slab), slab)
    theirs = pl.ds(pl.multiple_of((1 - c) * slab, slab), slab)
    nsend[...] = num[:, theirs, :].astype(BF16)
    ssend[...] = stat[:, theirs, :]
    swaps = []
    for n, (src, dst) in enumerate(((nsend, nrecv), (ssend, srecv))):
        swap = pltpu.make_async_remote_copy(
            src_ref=src, dst_ref=dst, send_sem=col_send.at[n], recv_sem=col_recv.at[n],
            device_id=(r, 1 - c), device_id_type=MESH,
        )
        swap.start()
        swaps.append(swap)
    for swap in swaps:
        swap.wait()
    own_stat = stat[:, mine, :]
    got_stat = srecv[...]
    top = jnp.maximum(own_stat[0], got_stat[0])
    own_scale = jnp.exp(own_stat[0] - top)
    got_scale = jnp.exp(got_stat[0] - top)
    inverse = 1.0 / (own_scale * own_stat[1] + got_scale * got_stat[1])
    own_scale = (own_scale * inverse)[None]
    got_scale = (got_scale * inverse)[None]
    wide_lanes = num.shape[2]
    step = 8

    @pl.loop(0, half // step)
    def _(n):
        part = pl.ds(n * step, step)
        norm = rows_ref[part, mine, :].reshape(step * slab, lanes)
        gate = jax.nn.sigmoid(dot_nn(norm, gate_ref[...]))
        mixed = own_scale * num[part, mine, :] + got_scale * nrecv[part].astype(F32)
        gated = gate * mixed.reshape(step * slab, wide_lanes)
        high = gated.astype(BF16)
        low = (gated - high.astype(F32)).astype(BF16)
        res = (dot_nn(high, out_ref[...]) + dot_nn(low, out_ref[...])).astype(BF16)
        res = res.reshape(step, slab, lanes)
        update_ref[part] = res[:, :, : lanes // 2]
        update_ref[pl.ds(half + n * step, step)] = res[:, :, lanes // 2 :]

    for part in range(parts):
        @pl.loop(1, rows_n)
        def _(k):
            turn(part, k).wait_send()
            source = lax.rem(r + k, rows_n)
            pltpu.make_async_remote_copy(
                src_ref=ready.at[part, pl.ds(0, slab)],
                dst_ref=turned_ref.at[
                    :, pl.ds(pl.multiple_of(source * rows + part * chunk, chunk), chunk), :
                ],
                send_sem=turn_send.at[part, k],
                recv_sem=turn_recv.at[part, source],
                device_id=(source, c),
                device_id_type=MESH,
            ).wait_recv()

        local_turn(part).wait()


def triangle_kernel(split_at, turned_ref, proj_ref, bias_ref, inputs_ref, edge_ref, edges):
    j = pl.program_id(0)
    slab = edge_ref.shape[1]
    block = turned_ref[0]
    projected = dot_nn(block, proj_ref[...])
    inputs_ref[0, :, :split_at] = projected[:, :split_at].astype(BF16)
    inputs_ref[0, :, split_at:] = jax.nn.sigmoid(projected[:, split_at:]).astype(BF16)
    padded = bias_ref.shape[0]
    bias_rows = dot_nt(bias_ref[...], block)
    for t in range(edges.shape[0]):
        edges.at[t][pl.ds(j, padded, stride=slab), :] = bias_rows[:, t * 128 : (t + 1) * 128]

    @pl.when(j == slab - 1)
    def _():
        for t in range(edges.shape[0]):
            kept = edges[t, : edge_ref.shape[0] * slab].astype(BF16)
            edge_ref[:, :, t * 128 : (t + 1) * 128] = kept.reshape(edge_ref.shape[:2] + (128,))


def two_fold(weight):
    zero = jnp.zeros_like(weight)
    return jnp.concatenate(
        [jnp.concatenate([weight, zero], axis=1), jnp.concatenate([zero, weight], axis=1)], axis=0
    )


def head_fold(weight, heads):
    width = weight.shape[1] // heads
    split = weight.reshape(weight.shape[0], heads, 1, width)
    zero = jnp.zeros_like(split)
    top = jnp.concatenate([split, zero], axis=2)
    low = jnp.concatenate([zero, split], axis=2)
    return jnp.concatenate([top, low], axis=0).reshape(2 * weight.shape[0], 2 * weight.shape[1])


def fast_device(
    alignment, pair_rep, outer_left, outer_right, outer_proj, outer_bias, average_value,
    average_gate, average_logit, average_out, triangle_proj, triangle_bias,
):
    rows_n = lax.axis_size("row")
    seqs, slab, channels = alignment.shape
    rows, tile, width = pair_rep.shape
    factor = outer_left.shape[1]
    heads = average_logit.shape[1]
    half = seqs // 2
    lanes = 2 * channels
    full = 2 * average_value.shape[1]
    vmem = pl.BlockSpec(memory_space=pltpu.VMEM)
    limit = 56 * 1024 * 1024
    dma = pltpu.SemaphoreType.DMA
    cols, row_norm = pl.pallas_call(
        functools.partial(gather_kernel, rows_n),
        out_shape=(
            jax.ShapeDtypeStruct((half, tile, lanes), BF16),
            jax.ShapeDtypeStruct((half, rows, lanes), BF16),
        ),
        in_specs=[vmem],
        out_specs=(vmem, vmem),
        scratch_shapes=[
            pltpu.VMEM((half, slab, lanes), BF16),
            dma((rows_n,)),
            dma((rows_n,)),
            dma((2,)),
        ],
        compiler_params=pltpu.CompilerParams(
            collective_id=0, has_side_effects=True, vmem_limit_bytes=limit
        ),
    )(alignment)
    scaled = outer_proj.reshape(factor, factor, width).transpose(2, 1, 0)
    scaled = scaled.reshape(width, factor * factor) * (1.0 / seqs)
    pair_new, alignment_update, turned = pl.pallas_call(
        functools.partial(pair_kernel, rows_n, heads),
        out_shape=(
            jax.ShapeDtypeStruct(pair_rep.shape, BF16),
            jax.ShapeDtypeStruct(alignment.shape, BF16),
            jax.ShapeDtypeStruct((slab, rows_n * rows, width), BF16),
        ),
        in_specs=[vmem] * 11,
        out_specs=(vmem, vmem, vmem),
        scratch_shapes=[
            pltpu.VMEM((tile // 128, seqs * factor, 128), F32),
            pltpu.VMEM((seqs, factor * tile), BF16),
            pltpu.VMEM((half * rows, lanes), F32),
            pltpu.VMEM((rows * factor, seqs), BF16),
            pltpu.VMEM((8, factor * factor, tile), BF16),
            pltpu.VMEM((tile * slab, width), F32),
            pltpu.VMEM((rows // slab, tile, slab, width), BF16),
            pltpu.VMEM((tile // 128, heads * rows, 128), F32),
            pltpu.VMEM((half, rows, full), F32),
            pltpu.VMEM((2, rows, full), F32),
            pltpu.VMEM((half, slab, full), BF16),
            pltpu.VMEM((half, slab, full), BF16),
            pltpu.VMEM((2, slab, full), F32),
            pltpu.VMEM((2, slab, full), F32),
            dma((rows // slab, rows_n)),
            dma((rows // slab, rows_n)),
            dma((rows // slab,)),
            dma((2,)),
            dma((2,)),
        ],
        compiler_params=pltpu.CompilerParams(
            collective_id=1, has_side_effects=True, vmem_limit_bytes=limit
        ),
    )(
        cols, row_norm, pair_rep, two_fold(outer_right.T), two_fold(outer_left.T), scaled,
        outer_bias.reshape(1, -1), head_fold(average_value, heads), head_fold(average_gate, heads),
        average_logit.T, head_fold(average_out.T, heads).T,
    )
    edge_heads = triangle_bias.shape[1]
    edge_weight = jnp.pad(triangle_bias.T, ((0, 8 - edge_heads), (0, 0)))
    total = rows_n * rows
    split_at = 3 * (triangle_proj.shape[1] // 4)
    triangle_inputs, edge_bias = pl.pallas_call(
        functools.partial(triangle_kernel, split_at),
        grid=(slab,),
        out_shape=(
            jax.ShapeDtypeStruct((slab, total, triangle_proj.shape[1]), BF16),
            jax.ShapeDtypeStruct((edge_heads, slab, total), BF16),
        ),
        in_specs=[
            pl.BlockSpec((1, total, width), lambda j: (j, 0, 0)),
            pl.BlockSpec(triangle_proj.shape, lambda j: (0, 0)),
            pl.BlockSpec(edge_weight.shape, lambda j: (0, 0)),
        ],
        out_specs=(
            pl.BlockSpec((1, total, triangle_proj.shape[1]), lambda j: (j, 0, 0)),
            pl.BlockSpec((edge_heads, slab, total), lambda j: (0, 0, 0)),
        ),
        scratch_shapes=[pltpu.VMEM((total // 128, 8 * slab, 128), F32)],
        compiler_params=pltpu.CompilerParams(vmem_limit_bytes=limit),
    )(turned, triangle_proj, edge_weight)
    return (pair_new, alignment_update, triangle_inputs, edge_bias)


def choose_device(alignment, pair_rep, *rest):
    rows_n, cols_n = lax.axis_size("row"), lax.axis_size("col")
    slab, rows, tile = alignment.shape[1], pair_rep.shape[0], pair_rep.shape[1]
    fits = cols_n == 2 and rows_n % 4 == 0 and slab % 16 == 0 and rows == 2 * slab
    fits = fits and tile == rows_n * slab and tile % 128 == 0
    chosen = fast_device if fits else per_device
    return chosen(alignment, pair_rep, *rest)


def solution(mesh):
    placed = (
        P(None, ("col", "row"), None),
        P("row", "col", None),
        P(),
        P(),
        P(),
        P(),
        P(),
        P(),
        P(),
        P(),
        P(),
        P(),
    )
    return jax.shard_map(
        choose_device,
        mesh=mesh,
        in_specs=placed,
        out_specs=(
            P("row", "col", None),
            P(None, ("row", "col"), None),
            P(("col", "row"), None, None),
            P(None, ("col", "row"), None),
        ),
        check_vma=False,
    )
```

```python
import functools
import jax
import jax.numpy as jnp
from jax import lax
from jax.sharding import PartitionSpec as P
from jax.experimental import pallas as pl
from jax.experimental.pallas import tpu as pltpu

MESH = pl.DeviceIdType.MESH
BF16 = jnp.bfloat16
F32 = jnp.float32
NT = (((1,), (1,)), ((), ()))


def broadcast(shard, axis, root):
    mine = lax.axis_index(axis) == root
    return lax.psum(jnp.where(mine, shard, jnp.zeros_like(shard)), axis)


def standardize(values):
    widened = values.astype(jnp.float32)
    centered = widened - jnp.mean(widened, axis=-1, keepdims=True)
    spread = jnp.mean(centered * centered, axis=-1, keepdims=True)
    return centered * lax.rsqrt(spread + 1e-05)


def per_device(
    alignment,
    pair_rep,
    outer_left,
    outer_right,
    outer_proj,
    outer_bias,
    average_value,
    average_gate,
    average_logit,
    average_out,
    triangle_proj,
    triangle_bias,
):
    row_devices = lax.axis_size("row")
    col_devices = lax.axis_size("col")
    local_row_index = lax.axis_index("row")
    col_index = lax.axis_index("col")
    sequence_count, slab_length, alignment_channel_width = alignment.shape
    row_window, cols_tile, pair_width = pair_rep.shape
    factor_width = outer_left.shape[1]
    head_count = average_logit.shape[1]
    value_width = average_value.shape[1]
    head_width = value_width // head_count
    alignment_layer_norm = standardize(alignment).astype(jnp.bfloat16)
    normalized_flat_rows = alignment_layer_norm.reshape(
        sequence_count, slab_length * alignment_channel_width
    )
    normalized_columns = lax.all_gather(normalized_flat_rows, "row", axis=1, tiled=True)
    norm_wide = normalized_columns.reshape(sequence_count, cols_tile, alignment_channel_width)
    right_cols = jnp.dot(norm_wide, outer_right, preferred_element_type=jnp.float32).astype(
        jnp.bfloat16
    )
    value_cols = jnp.dot(norm_wide, average_value, preferred_element_type=jnp.float32).astype(
        jnp.bfloat16
    )
    group_member_count = row_devices // col_devices
    start_position = local_row_index % group_member_count * (row_window * alignment_channel_width)
    local_rows = lax.dynamic_slice_in_dim(
        normalized_columns, start_position, row_window * alignment_channel_width, 1
    )
    norm_rows = broadcast(local_rows, "col", local_row_index // group_member_count).reshape(
        sequence_count, row_window, alignment_channel_width
    )
    left_rows = jnp.dot(norm_rows, outer_left, preferred_element_type=jnp.float32).astype(
        jnp.bfloat16
    )
    row_block = 8
    block_count = row_window // row_block
    left_blocks = jnp.transpose(
        left_rows.reshape(sequence_count, block_count, row_block * factor_width), (1, 0, 2)
    )
    right_flat = right_cols.reshape(sequence_count, cols_tile * factor_width)

    def pair_block(block_items):
        left_flat, pair_rows = block_items
        outer_sum = lax.dot_general(
            left_flat, right_flat, (((0,), (0,)), ((), ())), preferred_element_type=jnp.float32
        )
        outer_sum = jnp.transpose(
            outer_sum.reshape(row_block, factor_width, cols_tile, factor_width), (0, 2, 1, 3)
        )
        outer_mean = (
            outer_sum.reshape(row_block, cols_tile, factor_width * factor_width) / sequence_count
        ).astype(jnp.bfloat16)
        update = jnp.dot(outer_mean, outer_proj, preferred_element_type=jnp.float32)
        return (pair_rows.astype(jnp.float32) + update + outer_bias).astype(jnp.bfloat16)

    pair_new = lax.map(
        pair_block, (left_blocks, pair_rep.reshape(block_count, row_block, cols_tile, pair_width))
    )
    pair_new = pair_new.reshape(row_window, cols_tile, pair_width)
    pair_norm = standardize(pair_new).astype(jnp.bfloat16)
    logits = jnp.einsum("ijc,ch->hij", pair_norm, average_logit, preferred_element_type=jnp.float32)
    peak_values = lax.pmax(jnp.max(logits, axis=2), "col")
    weights = jnp.exp(logits - peak_values[:, :, None]).astype(jnp.bfloat16)
    denom_part = jnp.sum(weights.astype(jnp.float32), axis=2)
    value_heads = value_cols.reshape(sequence_count, cols_tile, head_count, head_width)
    numer_part = jnp.einsum(
        "hij,sjhc->ishc", weights, value_heads, preferred_element_type=jnp.float32
    )
    numer_part = numer_part.reshape(row_window, sequence_count, value_width)
    out_wide = average_out.astype(jnp.float32)
    numer_sub, denom_sub = (
        lax.psum_scatter(
            numer_part.astype(jnp.bfloat16), "col", scatter_dimension=0, tiled=True
        ).astype(jnp.float32),
        lax.psum_scatter(
            denom_part.astype(jnp.bfloat16), "col", scatter_dimension=1, tiled=True
        ).astype(jnp.float32),
    )
    sub_len = numer_sub.shape[0]
    norm_sub = lax.dynamic_slice_in_dim(norm_rows, col_index * sub_len, sub_len, 1)
    gate_vals = jax.nn.sigmoid(jnp.dot(norm_sub, average_gate, preferred_element_type=jnp.float32))
    gate_vals = gate_vals.reshape(sequence_count, sub_len, head_count, head_width)
    numer_moved = jnp.transpose(
        numer_sub.reshape(sub_len, sequence_count, head_count, head_width), (1, 0, 2, 3)
    )
    gated_vals = (gate_vals * numer_moved / jnp.transpose(denom_sub)[None, :, :, None]).reshape(
        sequence_count, sub_len, value_width
    )
    alignment_update = jnp.dot(gated_vals, out_wide, precision=lax.Precision.HIGHEST).astype(
        jnp.bfloat16
    )
    piece_len = cols_tile // row_devices
    shaped = pair_norm.reshape(row_window, row_devices, piece_len, pair_width)
    split_at = 3 * (triangle_proj.shape[1] // 4)
    turned = lax.all_to_all(shaped, "row", split_axis=1, concat_axis=0, tiled=True)[:, 0]
    projected = jnp.einsum("jic,cd->ijd", turned, triangle_proj, preferred_element_type=jnp.float32)
    inputs = jnp.concatenate(
        [projected[..., :split_at], jax.nn.sigmoid(projected[..., split_at:])], axis=-1
    ).astype(jnp.bfloat16)
    bias_rows = jnp.einsum(
        "jic,ch->ihj", turned, triangle_bias, preferred_element_type=jnp.float32
    ).astype(jnp.bfloat16)
    triangle_inputs, bias_rows = (inputs, bias_rows)
    edge_bias = jnp.transpose(bias_rows, (1, 0, 2))
    return (pair_new, alignment_update, triangle_inputs, edge_bias)


def dot_nt(a, b):
    return lax.dot_general(a, b, NT, preferred_element_type=F32)


def dot_nn(a, b):
    return jnp.dot(a, b, preferred_element_type=F32)


def two_fold(weight, ref):
    wide = weight.astype(F32)
    zero = jnp.zeros_like(wide)
    tall, across = weight.shape
    ref[:tall] = jnp.concatenate([wide, zero], axis=1).astype(BF16)
    ref[tall:] = jnp.concatenate([zero, wide], axis=1).astype(BF16)


def fused_kernel(
    rows_n, heads, align_ref, pair_hbm, right_ref, left_ref, proj_ref, bias_ref, value_ref,
    gate_ref, logit_ref, out_ref, new_ref, update_ref, turned_ref, own, cols_ref, rows_ref,
    pair_ref, fresh_ref, right_w, left_w, value_w, gate_w, out_w, proj_wide, proj_back, proj_w,
    rs, rb, nr, lt, outer, spun, ready, lg, num, stat, nsend, nrecv, ssend, srecv, send_sem,
    recv_sem, row_sem, turn_send, turn_recv, local_sem, col_send, col_recv,
):
    half, tile, lanes = cols_ref.shape
    rows = rows_ref.shape[1]
    slab = tile // rows_n
    width = right_ref.shape[0]
    block = 8
    chunk = slab
    r, c = lax.axis_index("row"), lax.axis_index("col")
    far = rows_n // 4
    a, b, e = r // 4, (r // 2) % 2, r % 2

    def place(a_, b_, e_):
        return (a_ * 4 + b_ * 2 + e_, c)

    across = (a, 1 - b, e)
    beside = (a, b, 1 - e)
    distant = [(lax.rem(a + k, far), b, e) for k in range(1, far)]
    shard = c * rows_n + r
    owner = (shard // 2, 1 - c)
    source_col = (2 * r) // rows_n
    source_row = lax.rem(2 * r, rows_n)
    barrier = pltpu.get_barrier_semaphore()
    pair_load = pltpu.make_async_copy(pair_hbm, pair_ref, local_sem.at[0])
    pair_load.start()

    @pl.loop(1, rows_n)
    def _(k):
        pl.semaphore_signal(
            barrier, inc=1, device_id=(lax.rem(r + k, rows_n), c), device_id_type=MESH
        )

    pl.semaphore_signal(barrier, inc=1, device_id=(r, 1 - c), device_id_type=MESH)

    @pl.when(source_col != c)
    def _():
        for k in range(2):
            pl.semaphore_signal(
                barrier, inc=1, device_id=(source_row + k, source_col), device_id_type=MESH
            )

    wide = align_ref[...].astype(F32)
    centered = wide - jnp.mean(wide, axis=-1, keepdims=True)
    spread = jnp.mean(centered * centered, axis=-1, keepdims=True)
    norm = centered * lax.rsqrt(spread + 1e-05)
    own[...] = jnp.concatenate([norm[:half], norm[half:]], axis=-1).astype(BF16)
    pl.semaphore_wait(barrier, rows_n + 1)

    def window(index):
        return cols_ref.at[:, pl.ds(pl.multiple_of(index * slab, slab), slab), :]

    started = []

    def send(src, index, target):
        copy = pltpu.make_async_remote_copy(
            src_ref=src,
            dst_ref=window(index),
            send_sem=send_sem.at[len(started)],
            recv_sem=recv_sem.at[index],
            device_id=target,
            device_id_type=MESH,
        )
        copy.start()
        started.append(copy)

    def arrived(index):
        pltpu.make_async_remote_copy(
            src_ref=own,
            dst_ref=window(index),
            send_sem=send_sem.at[0],
            recv_sem=recv_sem.at[index],
            device_id=place(*beside),
            device_id_type=MESH,
        ).wait_recv()

    for spot in distant:
        send(own, r, place(*spot))
    send(own, r, place(*across))
    send(own, r, place(*beside))
    row_copy = pltpu.make_async_remote_copy(
        src_ref=own,
        dst_ref=rows_ref.at[:, pl.ds(pl.multiple_of(lax.rem(shard, 2) * slab, slab), slab), :],
        send_sem=send_sem.at[len(started)],
        recv_sem=row_sem.at[lax.rem(shard, 2)],
        device_id=owner,
        device_id_type=MESH,
    )
    row_copy.start()
    started.append(row_copy)
    window(r)[...] = own[...]
    two_fold(right_ref[...], right_w)
    two_fold(left_ref[...], left_w)
    two_fold(value_ref[...], value_w)
    two_fold(gate_ref[...], gate_w)
    two_fold(out_ref[...], out_w)
    proj_wide[...] = proj_ref[...].astype(F32) * (1.0 / (2 * half))
    for d in range(width):
        turned_rows = proj_wide[pl.ds(d, width, stride=width), :]
        proj_back[d * width : (d + 1) * width, :] = turned_rows
    proj_w[...] = proj_back[...].T.astype(BF16)

    def index_of(spot):
        return spot[0] * 4 + spot[1] * 2 + spot[2]

    def forward(spot, both):
        index = index_of(spot)
        arrived(index)
        if both:
            send(window(index), index, place(*across))
        send(window(index), index, place(*beside))

    forward(across, False)
    for k in range(far - 1, 0, -1):
        spot = (lax.rem(a + k, far), b, e)
        forward(spot, True)
    for k in range(far - 1, 0, -1):
        forward((lax.rem(a + k, far), 1 - b, e), False)
    for k in [0] + list(range(far - 1, 0, -1)):
        for flip in range(2):
            arrived(index_of((lax.rem(a + k, far), b if flip == 0 else 1 - b, 1 - e)))

    @pl.when(source_col == c)
    def _():
        rows_ref[...] = cols_ref[
            :, pl.ds(pl.multiple_of(source_row * slab, 2 * slab), 2 * slab), :
        ]

    @pl.when(source_col != c)
    def _():
        for k in range(2):
            pltpu.make_async_remote_copy(
                src_ref=own,
                dst_ref=rows_ref.at[:, k * slab : (k + 1) * slab, :],
                send_sem=send_sem.at[0],
                recv_sem=row_sem.at[k],
                device_id=owner,
                device_id_type=MESH,
            ).wait_recv()

    @pl.loop(0, half, unroll=8)
    def _(s):
        res = dot_nt(right_w[...], cols_ref[s])
        for t in range(tile // 128):
            piece = res[:, t * 128 : (t + 1) * 128]
            rs[t, pl.ds(pl.multiple_of(s * width, width), width), :] = piece[:width]
            rs[t, pl.ds(pl.multiple_of((half + s) * width, width), width), :] = piece[width:]

    for d in range(width):
        for t in range(tile // 128):
            at = d * tile + t * 128
            rb[:, at : at + 128] = rs.at[t][pl.ds(d, 2 * half, stride=width), :].astype(BF16)

    nr[...] = rows_ref[...].astype(F32).reshape(half * rows, lanes)
    tokens = jnp.concatenate(
        [nr[pl.ds(i, half, stride=rows), :].astype(BF16) for i in range(rows)], axis=0
    )
    left_all = dot_nt(left_w[...], tokens)
    for i in range(rows):
        res = left_all[:, i * half : (i + 1) * half]
        lt[i * width : (i + 1) * width, :] = jnp.concatenate(
            [res[:width], res[width:]], axis=1
        ).astype(BF16)

    pair_load.wait()

    def do_block(base, place):
        left = lt[pl.ds(pl.multiple_of(base * width, block * width), block * width), :]
        for d in range(width):
            res = dot_nn(left, rb[:, d * tile : (d + 1) * tile]).astype(BF16)
            outer[:, d * width : (d + 1) * width, :] = res.reshape(block, width, tile)

        for k in range(block):
            i = base + k
            update = dot_nn(proj_w[...], outer[k]).T
            fresh = (pair_ref[i].astype(F32) + update + bias_ref[...]).astype(BF16)
            fresh_ref[i] = fresh
            wide = fresh.astype(F32)
            centered = wide - jnp.mean(wide, axis=-1, keepdims=True)
            spread = jnp.mean(centered * centered, axis=-1, keepdims=True)
            norm = (centered * lax.rsqrt(spread + 1e-05)).astype(BF16)
            logit = dot_nt(logit_ref[...], norm)
            for t in range(tile // 128):
                lg.at[t][pl.ds(i, heads, stride=rows), :] = logit[:, t * 128 : (t + 1) * 128]
            spun[pl.ds(place + k, tile, stride=chunk), :] = norm.astype(F32)

    def turn(part, k):
        other = lax.rem(r + k, rows_n)
        return pltpu.make_async_remote_copy(
            src_ref=ready.at[part, pl.ds(other * slab, slab)],
            dst_ref=turned_ref.at[
                :, pl.ds(pl.multiple_of(r * rows + part * chunk, chunk), chunk), :
            ],
            send_sem=turn_send.at[part, k],
            recv_sem=turn_recv.at[part, r],
            device_id=(other, c),
            device_id_type=MESH,
        )

    def local_turn(part):
        return pltpu.make_async_copy(
            ready.at[part, pl.ds(r * slab, slab)],
            turned_ref.at[:, pl.ds(pl.multiple_of(r * rows + part * chunk, chunk), chunk), :],
            local_sem.at[1 + part],
        )

    parts = rows // chunk
    for part in range(parts):
        @pl.loop(0, chunk // block)
        def _(n):
            do_block(part * chunk + n * block, n * block)

        ready[part] = spun[...].astype(BF16).reshape(tile, chunk, lanes)
        local_turn(part).start()

        @pl.loop(1, rows_n)
        def _(k):
            turn(part, k).start()

    new_store = pltpu.make_async_copy(fresh_ref, new_ref, local_sem.at[0])
    new_store.start()
    logits = jnp.concatenate([lg[t] for t in range(tile // 128)], axis=1)
    peak = jnp.max(logits, axis=-1, keepdims=True)
    weights = jnp.exp(logits - peak).astype(BF16)
    groups = 2
    heads_in = heads // groups
    gspan = heads_in * rows
    wide_lanes = num.shape[2]
    glanes = wide_lanes // groups
    part_lanes = glanes // 2
    each = part_lanes // heads_in

    def pick(res):
        lane = lax.broadcasted_iota(jnp.int32, (rows, glanes), 1) % part_lanes
        total = res[:rows]
        for h in range(1, heads_in):
            total = jnp.where(lane >= h * each, res[h * rows : (h + 1) * rows], total)
        return total

    def spots(g):
        return [(g * part_lanes, 0), (wide_lanes // 2 + g * part_lanes, part_lanes)]

    def put(ref, index, g, res):
        for at, start in spots(g):
            ref[index, :, at : at + part_lanes] = res[:, start : start + part_lanes]

    ones = jnp.ones((tile, glanes), BF16)
    for g in range(groups):
        put(stat, 0, g, pick(jnp.broadcast_to(peak[g * gspan : (g + 1) * gspan], (gspan, glanes))))
        put(stat, 1, g, pick(dot_nn(weights[g * gspan : (g + 1) * gspan], ones)))

    @pl.loop(0, half, unroll=4)
    def _(s):
        values = dot_nn(cols_ref[s], value_w[...]).astype(BF16)
        for g in range(groups):
            chosen = jnp.concatenate([values[:, at : at + part_lanes] for at, _ in spots(g)], axis=1)
            put(num, s, g, pick(dot_nn(weights[g * gspan : (g + 1) * gspan], chosen)))

    mine = pl.ds(pl.multiple_of(c * slab, slab), slab)
    theirs = pl.ds(pl.multiple_of((1 - c) * slab, slab), slab)
    nsend[...] = num[:, theirs, :].astype(BF16)
    ssend[...] = stat[:, theirs, :]
    swaps = []
    for n, (src, dst) in enumerate(((nsend, nrecv), (ssend, srecv))):
        swap = pltpu.make_async_remote_copy(
            src_ref=src, dst_ref=dst, send_sem=col_send.at[n], recv_sem=col_recv.at[n],
            device_id=(r, 1 - c), device_id_type=MESH,
        )
        swap.start()
        swaps.append(swap)
    for swap in swaps:
        swap.wait()
    own_stat = stat[:, mine, :]
    got_stat = srecv[...]
    top = jnp.maximum(own_stat[0], got_stat[0])
    own_scale = jnp.exp(own_stat[0] - top)
    got_scale = jnp.exp(got_stat[0] - top)
    inverse = 1.0 / (own_scale * own_stat[1] + got_scale * got_stat[1])
    own_scale = (own_scale * inverse)[None]
    got_scale = (got_scale * inverse)[None]
    step = 8

    @pl.loop(0, half // step)
    def _(n):
        part = pl.ds(n * step, step)
        norm = rows_ref[part, mine, :].reshape(step * slab, lanes)
        gate = jax.nn.sigmoid(dot_nn(norm, gate_w[...]))
        mixed = own_scale * num[part, mine, :] + got_scale * nrecv[part].astype(F32)
        gated = gate * mixed.reshape(step * slab, wide_lanes)
        high = gated.astype(BF16)
        low = (gated - high.astype(F32)).astype(BF16)
        res = (dot_nt(high, out_w[...]) + dot_nt(low, out_w[...])).astype(BF16)
        res = res.reshape(step, slab, lanes)
        update_ref[part] = res[:, :, : lanes // 2]
        update_ref[pl.ds(half + n * step, step)] = res[:, :, lanes // 2 :]

    for part in range(parts):
        @pl.loop(1, rows_n)
        def _(k):
            turn(part, k).wait_send()
            source = lax.rem(r + k, rows_n)
            pltpu.make_async_remote_copy(
                src_ref=ready.at[part, pl.ds(0, slab)],
                dst_ref=turned_ref.at[
                    :, pl.ds(pl.multiple_of(source * rows + part * chunk, chunk), chunk), :
                ],
                send_sem=turn_send.at[part, k],
                recv_sem=turn_recv.at[part, source],
                device_id=(source, c),
                device_id_type=MESH,
            ).wait_recv()

        local_turn(part).wait()
    new_store.wait()
    for copy in started:
        copy.wait_send()


def triangle_kernel(split_at, turned_ref, proj_ref, bias_ref, inputs_ref, edge_ref, edges):
    j = pl.program_id(0)
    slab = edge_ref.shape[1]
    group = turned_ref.shape[0]
    edge_heads = bias_ref.shape[0]
    for n in range(group):
        block = turned_ref[n]
        projected = dot_nn(block, proj_ref[...])
        inputs_ref[n, :, :split_at] = projected[:, :split_at].astype(BF16)
        inputs_ref[n, :, split_at:] = jax.nn.sigmoid(projected[:, split_at:]).astype(BF16)
        bias_rows = dot_nt(bias_ref[...], block)
        for t in range(edges.shape[0]):
            piece = bias_rows[:, t * 128 : (t + 1) * 128]
            edges.at[t][pl.ds(j * group + n, edge_heads, stride=slab), :] = piece

    @pl.when(j == slab // group - 1)
    def _():
        for t in range(edges.shape[0]):
            kept = edges[t, : edge_ref.shape[0] * slab].astype(BF16)
            edge_ref[:, :, t * 128 : (t + 1) * 128] = kept.reshape(edge_ref.shape[:2] + (128,))


def fast_device(
    alignment, pair_rep, outer_left, outer_right, outer_proj, outer_bias, average_value,
    average_gate, average_logit, average_out, triangle_proj, triangle_bias,
):
    rows_n = lax.axis_size("row")
    seqs, slab, channels = alignment.shape
    rows, tile, width = pair_rep.shape
    factor = outer_left.shape[1]
    heads = average_logit.shape[1]
    half = seqs // 2
    lanes = 2 * channels
    full = 2 * average_value.shape[1]
    vmem = pl.BlockSpec(memory_space=pltpu.VMEM)
    limit = 56 * 1024 * 1024
    dma = pltpu.SemaphoreType.DMA
    anywhere = pl.BlockSpec(memory_space=pl.ANY)
    parts = rows // slab
    pair_new, alignment_update, turned = pl.pallas_call(
        functools.partial(fused_kernel, rows_n, heads),
        out_shape=(
            jax.ShapeDtypeStruct(pair_rep.shape, BF16),
            jax.ShapeDtypeStruct(alignment.shape, BF16),
            jax.ShapeDtypeStruct((slab, rows_n * rows, width), BF16),
        ),
        in_specs=[vmem, anywhere] + [vmem] * 8,
        out_specs=(anywhere, vmem, anywhere),
        scratch_shapes=[
            pltpu.VMEM((half, slab, lanes), BF16),
            pltpu.VMEM((half, tile, lanes), BF16),
            pltpu.VMEM((half, rows, lanes), BF16),
            pltpu.VMEM(pair_rep.shape, BF16),
            pltpu.VMEM(pair_rep.shape, BF16),
            pltpu.VMEM((2 * factor, lanes), BF16),
            pltpu.VMEM((2 * factor, lanes), BF16),
            pltpu.VMEM((lanes, full), BF16),
            pltpu.VMEM((lanes, full), BF16),
            pltpu.VMEM((lanes, full), BF16),
            pltpu.VMEM((factor * factor, width), F32),
            pltpu.VMEM((factor * factor, width), F32),
            pltpu.VMEM((width, factor * factor), BF16),
            pltpu.VMEM((tile // 128, seqs * factor, 128), F32),
            pltpu.VMEM((seqs, factor * tile), BF16),
            pltpu.VMEM((half * rows, lanes), F32),
            pltpu.VMEM((rows * factor, seqs), BF16),
            pltpu.VMEM((8, factor * factor, tile), BF16),
            pltpu.VMEM((tile * slab, width), F32),
            pltpu.VMEM((parts, tile, slab, width), BF16),
            pltpu.VMEM((tile // 128, heads * rows, 128), F32),
            pltpu.VMEM((half, rows, full), F32),
            pltpu.VMEM((2, rows, full), F32),
            pltpu.VMEM((half, slab, full), BF16),
            pltpu.VMEM((half, slab, full), BF16),
            pltpu.VMEM((2, slab, full), F32),
            pltpu.VMEM((2, slab, full), F32),
            dma((rows_n,)),
            dma((rows_n,)),
            dma((2,)),
            dma((parts, rows_n)),
            dma((parts, rows_n)),
            dma((1 + parts,)),
            dma((2,)),
            dma((2,)),
        ],
        compiler_params=pltpu.CompilerParams(
            collective_id=0, has_side_effects=True, vmem_limit_bytes=limit
        ),
    )(
        alignment, pair_rep, outer_right.T, outer_left.T, outer_proj, outer_bias.reshape(1, -1),
        average_value, average_gate, average_logit.T, average_out.T,
    )
    edge_heads = triangle_bias.shape[1]
    edge_weight = triangle_bias.T
    group = 4
    total = rows_n * rows
    split_at = 3 * (triangle_proj.shape[1] // 4)
    triangle_inputs, edge_bias = pl.pallas_call(
        functools.partial(triangle_kernel, split_at),
        grid=(slab // group,),
        out_shape=(
            jax.ShapeDtypeStruct((slab, total, triangle_proj.shape[1]), BF16),
            jax.ShapeDtypeStruct((edge_heads, slab, total), BF16),
        ),
        in_specs=[
            pl.BlockSpec((group, total, width), lambda j: (j, 0, 0)),
            pl.BlockSpec(triangle_proj.shape, lambda j: (0, 0)),
            pl.BlockSpec(edge_weight.shape, lambda j: (0, 0)),
        ],
        out_specs=(
            pl.BlockSpec((group, total, triangle_proj.shape[1]), lambda j: (j, 0, 0)),
            pl.BlockSpec((edge_heads, slab, total), lambda j: (0, 0, 0)),
        ),
        scratch_shapes=[pltpu.VMEM((total // 128, edge_heads * slab, 128), F32)],
        compiler_params=pltpu.CompilerParams(vmem_limit_bytes=limit),
    )(turned, triangle_proj, edge_weight)
    return (pair_new, alignment_update, triangle_inputs, edge_bias)


def choose_device(alignment, pair_rep, *rest):
    rows_n, cols_n = lax.axis_size("row"), lax.axis_size("col")
    slab, rows, tile = alignment.shape[1], pair_rep.shape[0], pair_rep.shape[1]
    fits = cols_n == 2 and rows_n % 4 == 0 and slab % 16 == 0 and rows == 2 * slab
    seqs = alignment.shape[0]
    fits = fits and tile == rows_n * slab and tile % 128 == 0 and seqs & (seqs - 1) == 0
    chosen = fast_device if fits else per_device
    return chosen(alignment, pair_rep, *rest)


def solution(mesh):
    placed = (
        P(None, ("col", "row"), None),
        P("row", "col", None),
        P(),
        P(),
        P(),
        P(),
        P(),
        P(),
        P(),
        P(),
        P(),
        P(),
    )
    return jax.shard_map(
        choose_device,
        mesh=mesh,
        in_specs=placed,
        out_specs=(
            P("row", "col", None),
            P(None, ("row", "col"), None),
            P(("col", "row"), None, None),
            P(None, ("col", "row"), None),
        ),
        check_vma=False,
    )
```

```python
import functools
import jax
import jax.numpy as jnp
from jax import lax
from jax.sharding import PartitionSpec as P
from jax.experimental import pallas as pl
from jax.experimental.pallas import tpu as pltpu

MESH = pl.DeviceIdType.MESH
BF16 = jnp.bfloat16
F32 = jnp.float32
NT = (((1,), (1,)), ((), ()))


def broadcast(shard, axis, root):
    mine = lax.axis_index(axis) == root
    return lax.psum(jnp.where(mine, shard, jnp.zeros_like(shard)), axis)


def standardize(values):
    widened = values.astype(jnp.float32)
    centered = widened - jnp.mean(widened, axis=-1, keepdims=True)
    spread = jnp.mean(centered * centered, axis=-1, keepdims=True)
    return centered * lax.rsqrt(spread + 1e-05)


def per_device(
    alignment,
    pair_rep,
    outer_left,
    outer_right,
    outer_proj,
    outer_bias,
    average_value,
    average_gate,
    average_logit,
    average_out,
    triangle_proj,
    triangle_bias,
):
    row_devices = lax.axis_size("row")
    col_devices = lax.axis_size("col")
    local_row_index = lax.axis_index("row")
    col_index = lax.axis_index("col")
    sequence_count, slab_length, alignment_channel_width = alignment.shape
    row_window, cols_tile, pair_width = pair_rep.shape
    factor_width = outer_left.shape[1]
    head_count = average_logit.shape[1]
    value_width = average_value.shape[1]
    head_width = value_width // head_count
    alignment_layer_norm = standardize(alignment).astype(jnp.bfloat16)
    normalized_flat_rows = alignment_layer_norm.reshape(
        sequence_count, slab_length * alignment_channel_width
    )
    normalized_columns = lax.all_gather(normalized_flat_rows, "row", axis=1, tiled=True)
    norm_wide = normalized_columns.reshape(sequence_count, cols_tile, alignment_channel_width)
    right_cols = jnp.dot(norm_wide, outer_right, preferred_element_type=jnp.float32).astype(
        jnp.bfloat16
    )
    value_cols = jnp.dot(norm_wide, average_value, preferred_element_type=jnp.float32).astype(
        jnp.bfloat16
    )
    group_member_count = row_devices // col_devices
    start_position = local_row_index % group_member_count * (row_window * alignment_channel_width)
    local_rows = lax.dynamic_slice_in_dim(
        normalized_columns, start_position, row_window * alignment_channel_width, 1
    )
    norm_rows = broadcast(local_rows, "col", local_row_index // group_member_count).reshape(
        sequence_count, row_window, alignment_channel_width
    )
    left_rows = jnp.dot(norm_rows, outer_left, preferred_element_type=jnp.float32).astype(
        jnp.bfloat16
    )
    row_block = 8
    block_count = row_window // row_block
    left_blocks = jnp.transpose(
        left_rows.reshape(sequence_count, block_count, row_block * factor_width), (1, 0, 2)
    )
    right_flat = right_cols.reshape(sequence_count, cols_tile * factor_width)

    def pair_block(block_items):
        left_flat, pair_rows = block_items
        outer_sum = lax.dot_general(
            left_flat, right_flat, (((0,), (0,)), ((), ())), preferred_element_type=jnp.float32
        )
        outer_sum = jnp.transpose(
            outer_sum.reshape(row_block, factor_width, cols_tile, factor_width), (0, 2, 1, 3)
        )
        outer_mean = (
            outer_sum.reshape(row_block, cols_tile, factor_width * factor_width) / sequence_count
        ).astype(jnp.bfloat16)
        update = jnp.dot(outer_mean, outer_proj, preferred_element_type=jnp.float32)
        return (pair_rows.astype(jnp.float32) + update + outer_bias).astype(jnp.bfloat16)

    pair_new = lax.map(
        pair_block, (left_blocks, pair_rep.reshape(block_count, row_block, cols_tile, pair_width))
    )
    pair_new = pair_new.reshape(row_window, cols_tile, pair_width)
    pair_norm = standardize(pair_new).astype(jnp.bfloat16)
    logits = jnp.einsum("ijc,ch->hij", pair_norm, average_logit, preferred_element_type=jnp.float32)
    peak_values = lax.pmax(jnp.max(logits, axis=2), "col")
    weights = jnp.exp(logits - peak_values[:, :, None]).astype(jnp.bfloat16)
    denom_part = jnp.sum(weights.astype(jnp.float32), axis=2)
    value_heads = value_cols.reshape(sequence_count, cols_tile, head_count, head_width)
    numer_part = jnp.einsum(
        "hij,sjhc->ishc", weights, value_heads, preferred_element_type=jnp.float32
    )
    numer_part = numer_part.reshape(row_window, sequence_count, value_width)
    out_wide = average_out.astype(jnp.float32)
    numer_sub, denom_sub = (
        lax.psum_scatter(
            numer_part.astype(jnp.bfloat16), "col", scatter_dimension=0, tiled=True
        ).astype(jnp.float32),
        lax.psum_scatter(
            denom_part.astype(jnp.bfloat16), "col", scatter_dimension=1, tiled=True
        ).astype(jnp.float32),
    )
    sub_len = numer_sub.shape[0]
    norm_sub = lax.dynamic_slice_in_dim(norm_rows, col_index * sub_len, sub_len, 1)
    gate_vals = jax.nn.sigmoid(jnp.dot(norm_sub, average_gate, preferred_element_type=jnp.float32))
    gate_vals = gate_vals.reshape(sequence_count, sub_len, head_count, head_width)
    numer_moved = jnp.transpose(
        numer_sub.reshape(sub_len, sequence_count, head_count, head_width), (1, 0, 2, 3)
    )
    gated_vals = (gate_vals * numer_moved / jnp.transpose(denom_sub)[None, :, :, None]).reshape(
        sequence_count, sub_len, value_width
    )
    alignment_update = jnp.dot(gated_vals, out_wide, precision=lax.Precision.HIGHEST).astype(
        jnp.bfloat16
    )
    piece_len = cols_tile // row_devices
    shaped = pair_norm.reshape(row_window, row_devices, piece_len, pair_width)
    split_at = 3 * (triangle_proj.shape[1] // 4)
    turned = lax.all_to_all(shaped, "row", split_axis=1, concat_axis=0, tiled=True)[:, 0]
    projected = jnp.einsum("jic,cd->ijd", turned, triangle_proj, preferred_element_type=jnp.float32)
    inputs = jnp.concatenate(
        [projected[..., :split_at], jax.nn.sigmoid(projected[..., split_at:])], axis=-1
    ).astype(jnp.bfloat16)
    bias_rows = jnp.einsum(
        "jic,ch->ihj", turned, triangle_bias, preferred_element_type=jnp.float32
    ).astype(jnp.bfloat16)
    triangle_inputs, bias_rows = (inputs, bias_rows)
    edge_bias = jnp.transpose(bias_rows, (1, 0, 2))
    return (pair_new, alignment_update, triangle_inputs, edge_bias)


def dot_nt(a, b):
    return lax.dot_general(a, b, NT, preferred_element_type=F32)


def dot_nn(a, b):
    return jnp.dot(a, b, preferred_element_type=F32)


def two_fold(weight, ref):
    wide = weight.astype(F32)
    zero = jnp.zeros_like(wide)
    tall, across = weight.shape
    ref[:tall] = jnp.concatenate([wide, zero], axis=1).astype(BF16)
    ref[tall:] = jnp.concatenate([zero, wide], axis=1).astype(BF16)


def fused_kernel(
    rows_n, heads, align_ref, pair_hbm, right_ref, left_ref, proj_ref, bias_ref, value_ref,
    gate_ref, logit_ref, out_ref, new_ref, update_ref, turned_ref, own, cols_ref, rows_ref,
    pair_ref, fresh_ref, right_w, left_w, value_w, gate_w, out_w, proj_wide, proj_back, proj_w,
    rs, rb, nr, lt, outer, spun, ready, lg, num, stat, nsend, nrecv, ssend, srecv, send_sem,
    recv_sem, row_sem, turn_send, turn_recv, local_sem, col_send, col_recv,
):
    half, tile, lanes = cols_ref.shape
    rows = rows_ref.shape[1]
    slab = tile // rows_n
    width = right_ref.shape[0]
    block = 8
    chunk = slab
    r, c = lax.axis_index("row"), lax.axis_index("col")
    far = rows_n // 4
    a, b, e = r // 4, (r // 2) % 2, r % 2

    def place(a_, b_, e_):
        return (a_ * 4 + b_ * 2 + e_, c)

    across = (a, 1 - b, e)
    beside = (a, b, 1 - e)
    distant = [(lax.rem(a + k, far), b, e) for k in range(1, far)]
    shard = c * rows_n + r
    owner = (shard // 2, 1 - c)
    source_col = (2 * r) // rows_n
    source_row = lax.rem(2 * r, rows_n)
    barrier = pltpu.get_barrier_semaphore()
    pair_load = pltpu.make_async_copy(pair_hbm, pair_ref, local_sem.at[0])
    pair_load.start()

    @pl.loop(1, rows_n)
    def _(k):
        pl.semaphore_signal(
            barrier, inc=1, device_id=(lax.rem(r + k, rows_n), c), device_id_type=MESH
        )

    pl.semaphore_signal(barrier, inc=1, device_id=(r, 1 - c), device_id_type=MESH)

    @pl.when(source_col != c)
    def _():
        for k in range(2):
            pl.semaphore_signal(
                barrier, inc=1, device_id=(source_row + k, source_col), device_id_type=MESH
            )

    wide = align_ref[...].astype(F32)
    centered = wide - jnp.mean(wide, axis=-1, keepdims=True)
    spread = jnp.mean(centered * centered, axis=-1, keepdims=True)
    norm = centered * lax.rsqrt(spread + 1e-05)
    own[...] = jnp.concatenate([norm[:half], norm[half:]], axis=-1).astype(BF16)
    pl.semaphore_wait(barrier, rows_n + 1)

    def window(index):
        return cols_ref.at[:, pl.ds(pl.multiple_of(index * slab, slab), slab), :]

    started = []

    def send(src, index, target):
        copy = pltpu.make_async_remote_copy(
            src_ref=src,
            dst_ref=window(index),
            send_sem=send_sem.at[len(started)],
            recv_sem=recv_sem.at[index],
            device_id=target,
            device_id_type=MESH,
        )
        copy.start()
        started.append(copy)

    def arrived(index):
        pltpu.make_async_remote_copy(
            src_ref=own,
            dst_ref=window(index),
            send_sem=send_sem.at[0],
            recv_sem=recv_sem.at[index],
            device_id=place(*beside),
            device_id_type=MESH,
        ).wait_recv()

    for spot in distant:
        send(own, r, place(*spot))
    send(own, r, place(*across))
    send(own, r, place(*beside))
    row_copy = pltpu.make_async_remote_copy(
        src_ref=own,
        dst_ref=rows_ref.at[:, pl.ds(pl.multiple_of(lax.rem(shard, 2) * slab, slab), slab), :],
        send_sem=send_sem.at[len(started)],
        recv_sem=row_sem.at[lax.rem(shard, 2)],
        device_id=owner,
        device_id_type=MESH,
    )
    row_copy.start()
    started.append(row_copy)
    window(r)[...] = own[...]
    two_fold(right_ref[...], right_w)
    two_fold(left_ref[...], left_w)
    two_fold(value_ref[...], value_w)
    two_fold(gate_ref[...], gate_w)
    two_fold(out_ref[...], out_w)
    proj_wide[...] = proj_ref[...].astype(F32) * (1.0 / (2 * half))
    for d in range(width):
        turned_rows = proj_wide[pl.ds(d, width, stride=width), :]
        proj_back[d * width : (d + 1) * width, :] = turned_rows
    proj_w[...] = proj_back[...].T.astype(BF16)

    def index_of(spot):
        return spot[0] * 4 + spot[1] * 2 + spot[2]

    def forward(spot, both):
        index = index_of(spot)
        arrived(index)
        if both:
            send(window(index), index, place(*across))
        send(window(index), index, place(*beside))

    forward(across, False)
    for k in range(far - 1, 0, -1):
        spot = (lax.rem(a + k, far), b, e)
        forward(spot, True)
    for k in range(far - 1, 0, -1):
        forward((lax.rem(a + k, far), 1 - b, e), False)
    for k in [0] + list(range(far - 1, 0, -1)):
        for flip in range(2):
            arrived(index_of((lax.rem(a + k, far), b if flip == 0 else 1 - b, 1 - e)))

    @pl.when(source_col == c)
    def _():
        rows_ref[...] = cols_ref[
            :, pl.ds(pl.multiple_of(source_row * slab, 2 * slab), 2 * slab), :
        ]

    @pl.when(source_col != c)
    def _():
        for k in range(2):
            pltpu.make_async_remote_copy(
                src_ref=own,
                dst_ref=rows_ref.at[:, k * slab : (k + 1) * slab, :],
                send_sem=send_sem.at[0],
                recv_sem=row_sem.at[k],
                device_id=owner,
                device_id_type=MESH,
            ).wait_recv()

    @pl.loop(0, half, unroll=8)
    def _(s):
        res = dot_nt(right_w[...], cols_ref[s])
        for t in range(tile // 128):
            piece = res[:, t * 128 : (t + 1) * 128]
            rs[t, pl.ds(pl.multiple_of(s * width, width), width), :] = piece[:width]
            rs[t, pl.ds(pl.multiple_of((half + s) * width, width), width), :] = piece[width:]

    for d in range(width):
        for t in range(tile // 128):
            at = d * tile + t * 128
            rb[:, at : at + 128] = rs.at[t][pl.ds(d, 2 * half, stride=width), :].astype(BF16)

    nr[...] = rows_ref[...].astype(F32).reshape(half * rows, lanes)
    tokens = jnp.concatenate(
        [nr[pl.ds(i, half, stride=rows), :].astype(BF16) for i in range(rows)], axis=0
    )
    left_all = dot_nt(left_w[...], tokens)
    for i in range(rows):
        res = left_all[:, i * half : (i + 1) * half]
        lt[i * width : (i + 1) * width, :] = jnp.concatenate(
            [res[:width], res[width:]], axis=1
        ).astype(BF16)

    pair_load.wait()

    def do_block(base, place):
        left = lt[pl.ds(pl.multiple_of(base * width, block * width), block * width), :]
        for d in range(width):
            res = dot_nn(left, rb[:, d * tile : (d + 1) * tile]).astype(BF16)
            outer[:, d * width : (d + 1) * width, :] = res.reshape(block, width, tile)

        for k in range(block):
            i = base + k
            update = dot_nn(proj_w[...], outer[k]).T
            fresh = (pair_ref[i].astype(F32) + update + bias_ref[...]).astype(BF16)
            fresh_ref[i] = fresh
            wide = fresh.astype(F32)
            centered = wide - jnp.mean(wide, axis=-1, keepdims=True)
            spread = jnp.mean(centered * centered, axis=-1, keepdims=True)
            norm = (centered * lax.rsqrt(spread + 1e-05)).astype(BF16)
            logit = dot_nt(logit_ref[...], norm)
            for t in range(tile // 128):
                lg.at[t][pl.ds(i, heads, stride=rows), :] = logit[:, t * 128 : (t + 1) * 128]
            spun[pl.ds(place + k, tile, stride=chunk), :] = norm.astype(F32)

    def turn(part, k):
        other = lax.rem(r + k, rows_n)
        return pltpu.make_async_remote_copy(
            src_ref=ready.at[part, pl.ds(other * slab, slab)],
            dst_ref=turned_ref.at[
                :, pl.ds(pl.multiple_of(r * rows + part * chunk, chunk), chunk), :
            ],
            send_sem=turn_send.at[part, k],
            recv_sem=turn_recv.at[part, r],
            device_id=(other, c),
            device_id_type=MESH,
        )

    def local_turn(part):
        return pltpu.make_async_copy(
            ready.at[part, pl.ds(r * slab, slab)],
            turned_ref.at[:, pl.ds(pl.multiple_of(r * rows + part * chunk, chunk), chunk), :],
            local_sem.at[1 + part],
        )

    parts = rows // chunk
    for part in range(parts):
        @pl.loop(0, chunk // block)
        def _(n):
            do_block(part * chunk + n * block, n * block)

        ready[part] = spun[...].astype(BF16).reshape(tile, chunk, lanes)
        local_turn(part).start()

        @pl.loop(1, rows_n)
        def _(k):
            turn(part, lax.rem(k + rows_n // 2 - 2, rows_n - 1) + 1).start()

    new_store = pltpu.make_async_copy(fresh_ref, new_ref, local_sem.at[0])
    new_store.start()
    logits = jnp.concatenate([lg[t] for t in range(tile // 128)], axis=1)
    peak = jnp.max(logits, axis=-1, keepdims=True)
    weights = jnp.exp(logits - peak).astype(BF16)
    groups = 2
    heads_in = heads // groups
    gspan = heads_in * rows
    wide_lanes = num.shape[2]
    glanes = wide_lanes // groups
    part_lanes = glanes // 2
    each = part_lanes // heads_in

    def pick(res):
        lane = lax.broadcasted_iota(jnp.int32, (rows, glanes), 1) % part_lanes
        total = res[:rows]
        for h in range(1, heads_in):
            total = jnp.where(lane >= h * each, res[h * rows : (h + 1) * rows], total)
        return total

    def spots(g):
        return [(g * part_lanes, 0), (wide_lanes // 2 + g * part_lanes, part_lanes)]

    def put(ref, index, g, res):
        for at, start in spots(g):
            ref[index, :, at : at + part_lanes] = res[:, start : start + part_lanes]

    ones = jnp.ones((tile, glanes), BF16)
    for g in range(groups):
        put(stat, 0, g, pick(jnp.broadcast_to(peak[g * gspan : (g + 1) * gspan], (gspan, glanes))))
        put(stat, 1, g, pick(dot_nn(weights[g * gspan : (g + 1) * gspan], ones)))

    mine = pl.ds(pl.multiple_of(c * slab, slab), slab)
    theirs = pl.ds(pl.multiple_of((1 - c) * slab, slab), slab)
    step = 8

    def swap(src, dst, n):
        copy = pltpu.make_async_remote_copy(
            src_ref=src, dst_ref=dst, send_sem=col_send.at[n], recv_sem=col_recv.at[n],
            device_id=(r, 1 - c), device_id_type=MESH,
        )
        copy.start()
        return copy

    ssend[...] = stat[:, theirs, :]
    stat_swap = swap(ssend, srecv, half // step)
    swaps = []
    for n in range(half // step):
        @pl.loop(n * step, (n + 1) * step, unroll=4)
        def _(s):
            values = dot_nn(cols_ref[s], value_w[...]).astype(BF16)
            for g in range(groups):
                chosen = jnp.concatenate(
                    [values[:, at : at + part_lanes] for at, _ in spots(g)], axis=1
                )
                put(num, s, g, pick(dot_nn(weights[g * gspan : (g + 1) * gspan], chosen)))

        part = pl.ds(n * step, step)
        nsend[part] = num[part, theirs, :].astype(BF16)
        swaps.append(swap(nsend.at[part], nrecv.at[part], n))

    stat_swap.wait()
    own_stat = stat[:, mine, :]
    got_stat = srecv[...]
    top = jnp.maximum(own_stat[0], got_stat[0])
    own_scale = jnp.exp(own_stat[0] - top)
    got_scale = jnp.exp(got_stat[0] - top)
    inverse = 1.0 / (own_scale * own_stat[1] + got_scale * got_stat[1])
    own_scale = (own_scale * inverse)[None]
    got_scale = (got_scale * inverse)[None]

    for n in range(half // step):
        swaps[n].wait()
        part = pl.ds(n * step, step)
        norm = rows_ref[part, mine, :].reshape(step * slab, lanes)
        gate = jax.nn.sigmoid(dot_nn(norm, gate_w[...]))
        mixed = own_scale * num[part, mine, :] + got_scale * nrecv[part].astype(F32)
        gated = gate * mixed.reshape(step * slab, wide_lanes)
        high = gated.astype(BF16)
        low = (gated - high.astype(F32)).astype(BF16)
        res = (dot_nt(high, out_w[...]) + dot_nt(low, out_w[...])).astype(BF16)
        res = res.reshape(step, slab, lanes)
        update_ref[part] = res[:, :, : lanes // 2]
        update_ref[pl.ds(half + n * step, step)] = res[:, :, lanes // 2 :]

    for part in range(parts):
        @pl.loop(1, rows_n)
        def _(k):
            turn(part, k).wait_send()
            source = lax.rem(r + k, rows_n)
            pltpu.make_async_remote_copy(
                src_ref=ready.at[part, pl.ds(0, slab)],
                dst_ref=turned_ref.at[
                    :, pl.ds(pl.multiple_of(source * rows + part * chunk, chunk), chunk), :
                ],
                send_sem=turn_send.at[part, k],
                recv_sem=turn_recv.at[part, source],
                device_id=(source, c),
                device_id_type=MESH,
            ).wait_recv()

        local_turn(part).wait()
    new_store.wait()
    for copy in started:
        copy.wait_send()


def triangle_kernel(split_at, turned_ref, proj_ref, bias_ref, inputs_ref, edge_ref, edges):
    j = pl.program_id(0)
    slab = edge_ref.shape[1]
    group = turned_ref.shape[0]
    edge_heads = bias_ref.shape[0]
    for n in range(group):
        block = turned_ref[n]
        projected = dot_nn(block, proj_ref[...])
        inputs_ref[n, :, :split_at] = projected[:, :split_at].astype(BF16)
        inputs_ref[n, :, split_at:] = jax.nn.sigmoid(projected[:, split_at:]).astype(BF16)
        bias_rows = dot_nt(bias_ref[...], block)
        for t in range(edges.shape[0]):
            piece = bias_rows[:, t * 128 : (t + 1) * 128]
            edges.at[t][pl.ds(j * group + n, edge_heads, stride=slab), :] = piece

    @pl.when(j == slab // group - 1)
    def _():
        for t in range(edges.shape[0]):
            kept = edges[t, : edge_ref.shape[0] * slab].astype(BF16)
            edge_ref[:, :, t * 128 : (t + 1) * 128] = kept.reshape(edge_ref.shape[:2] + (128,))


def fast_device(
    alignment, pair_rep, outer_left, outer_right, outer_proj, outer_bias, average_value,
    average_gate, average_logit, average_out, triangle_proj, triangle_bias,
):
    rows_n = lax.axis_size("row")
    seqs, slab, channels = alignment.shape
    rows, tile, width = pair_rep.shape
    factor = outer_left.shape[1]
    heads = average_logit.shape[1]
    half = seqs // 2
    lanes = 2 * channels
    full = 2 * average_value.shape[1]
    vmem = pl.BlockSpec(memory_space=pltpu.VMEM)
    limit = 56 * 1024 * 1024
    dma = pltpu.SemaphoreType.DMA
    anywhere = pl.BlockSpec(memory_space=pl.ANY)
    parts = rows // slab
    pair_new, alignment_update, turned = pl.pallas_call(
        functools.partial(fused_kernel, rows_n, heads),
        out_shape=(
            jax.ShapeDtypeStruct(pair_rep.shape, BF16),
            jax.ShapeDtypeStruct(alignment.shape, BF16),
            jax.ShapeDtypeStruct((slab, rows_n * rows, width), BF16),
        ),
        in_specs=[vmem, anywhere] + [vmem] * 8,
        out_specs=(anywhere, vmem, anywhere),
        scratch_shapes=[
            pltpu.VMEM((half, slab, lanes), BF16),
            pltpu.VMEM((half, tile, lanes), BF16),
            pltpu.VMEM((half, rows, lanes), BF16),
            pltpu.VMEM(pair_rep.shape, BF16),
            pltpu.VMEM(pair_rep.shape, BF16),
            pltpu.VMEM((2 * factor, lanes), BF16),
            pltpu.VMEM((2 * factor, lanes), BF16),
            pltpu.VMEM((lanes, full), BF16),
            pltpu.VMEM((lanes, full), BF16),
            pltpu.VMEM((lanes, full), BF16),
            pltpu.VMEM((factor * factor, width), F32),
            pltpu.VMEM((factor * factor, width), F32),
            pltpu.VMEM((width, factor * factor), BF16),
            pltpu.VMEM((tile // 128, seqs * factor, 128), F32),
            pltpu.VMEM((seqs, factor * tile), BF16),
            pltpu.VMEM((half * rows, lanes), F32),
            pltpu.VMEM((rows * factor, seqs), BF16),
            pltpu.VMEM((8, factor * factor, tile), BF16),
            pltpu.VMEM((tile * slab, width), F32),
            pltpu.VMEM((parts, tile, slab, width), BF16),
            pltpu.VMEM((tile // 128, heads * rows, 128), F32),
            pltpu.VMEM((half, rows, full), F32),
            pltpu.VMEM((2, rows, full), F32),
            pltpu.VMEM((half, slab, full), BF16),
            pltpu.VMEM((half, slab, full), BF16),
            pltpu.VMEM((2, slab, full), F32),
            pltpu.VMEM((2, slab, full), F32),
            dma((rows_n,)),
            dma((rows_n,)),
            dma((2,)),
            dma((parts, rows_n)),
            dma((parts, rows_n)),
            dma((1 + parts,)),
            dma((1 + half // 8,)),
            dma((1 + half // 8,)),
        ],
        compiler_params=pltpu.CompilerParams(
            collective_id=0, has_side_effects=True, vmem_limit_bytes=limit
        ),
    )(
        alignment, pair_rep, outer_right.T, outer_left.T, outer_proj, outer_bias.reshape(1, -1),
        average_value, average_gate, average_logit.T, average_out.T,
    )
    edge_heads = triangle_bias.shape[1]
    edge_weight = triangle_bias.T
    group = 4
    total = rows_n * rows
    split_at = 3 * (triangle_proj.shape[1] // 4)
    triangle_inputs, edge_bias = pl.pallas_call(
        functools.partial(triangle_kernel, split_at),
        grid=(slab // group,),
        out_shape=(
            jax.ShapeDtypeStruct((slab, total, triangle_proj.shape[1]), BF16),
            jax.ShapeDtypeStruct((edge_heads, slab, total), BF16),
        ),
        in_specs=[
            pl.BlockSpec((group, total, width), lambda j: (j, 0, 0)),
            pl.BlockSpec(triangle_proj.shape, lambda j: (0, 0)),
            pl.BlockSpec(edge_weight.shape, lambda j: (0, 0)),
        ],
        out_specs=(
            pl.BlockSpec((group, total, triangle_proj.shape[1]), lambda j: (j, 0, 0)),
            pl.BlockSpec((edge_heads, slab, total), lambda j: (0, 0, 0)),
        ),
        scratch_shapes=[pltpu.VMEM((total // 128, edge_heads * slab, 128), F32)],
        compiler_params=pltpu.CompilerParams(vmem_limit_bytes=limit),
    )(turned, triangle_proj, edge_weight)
    return (pair_new, alignment_update, triangle_inputs, edge_bias)


def choose_device(alignment, pair_rep, *rest):
    rows_n, cols_n = lax.axis_size("row"), lax.axis_size("col")
    slab, rows, tile = alignment.shape[1], pair_rep.shape[0], pair_rep.shape[1]
    fits = cols_n == 2 and rows_n % 4 == 0 and slab % 16 == 0 and rows == 2 * slab
    seqs = alignment.shape[0]
    fits = fits and tile == rows_n * slab and tile % 128 == 0 and seqs & (seqs - 1) == 0
    chosen = fast_device if fits else per_device
    return chosen(alignment, pair_rep, *rest)


def solution(mesh):
    placed = (
        P(None, ("col", "row"), None),
        P("row", "col", None),
        P(),
        P(),
        P(),
        P(),
        P(),
        P(),
        P(),
        P(),
        P(),
        P(),
    )
    return jax.shard_map(
        choose_device,
        mesh=mesh,
        in_specs=placed,
        out_specs=(
            P("row", "col", None),
            P(None, ("row", "col"), None),
            P(("col", "row"), None, None),
            P(None, ("col", "row"), None),
        ),
        check_vma=False,
    )
```
